512 devices in a mesh: dp: 8 (over z), fsdp: 64 (over y, x, core).
Axes of the slice: x: 4, y: 8, z: 8, core: 2. Of those that a mesh axis runs over, the one named last changes fastest.
Arguments:
- gradients: bfloat16 [8, 512, 512, 512], P('dp', 'fsdp'), may hold values from -48 to 48
- owners: int32 [8, 64], P('dp'), may hold values from 0 to 63, as said below
Outputs:
- updates: bfloat16 [512, 512, 512], P('fsdp', 'dp')
- owner_scales: float32 [8, 64, 2], P('dp', 'fsdp')
The draws below stay inside these ranges and needn't reach their ends.
Inputs may be any that keep to these rules, and one draw needn't show every extreme that they name: Each entry names the owner of that block among the fsdp indices; no owner holds more than 2 blocks of a group, and in every group some owners hold exactly 2.
All inputs are finite; a program needn't handle non-finite values.
Results may differ from the reference program's by a relative error of at most 0.02.
Values may be sent and summed in bfloat16 or wider, within the bound.
A program may use at most 64 MiB of HBM per device.

```python
import math
import jax
import jax.numpy as jnp
from jax import lax

B = 512
MOST = 2
NBD = 64
NB = 512
N_DP = 8
N_FSDP = 64


def draw_gradients(key, part):
    key = jax.random.fold_in(key, 3)
    key_noise = jax.random.fold_in(key, 0)
    key_shape = jax.random.fold_in(key, 4)
    key_spread = jax.random.fold_in(key, 5)
    noise = jnp.clip(jax.random.normal(key_noise, (NB // NBD, B, NB, B), jnp.float32), -6.0, 6.0)
    spread = 0.3 + jax.random.uniform(key_spread, (1, 1, NB, 1), jnp.float32) * (math.log(30.0) - 0.3)
    column_shape = jnp.exp(-jax.random.uniform(key_shape, (1, 1, NB, B), jnp.float32) * spread)
    values = noise * column_shape
    return values.astype(jnp.bfloat16)


def draw_owners(key, part):
    key = jax.random.fold_in(key, 7)
    group_keys = jax.random.split(key, NB // NBD)

    def one_group(group_key):
        key_devices, key_order = jax.random.split(group_key)
        devices = jax.random.permutation(key_devices, N_FSDP)
        quarter = NBD // 4
        position = jnp.arange(NBD, dtype=jnp.int32)
        doubled = devices[position // 2]
        single = devices[jnp.clip(position - quarter, 0, N_FSDP - 1)]
        copies = jnp.where(position < 2 * quarter, doubled, single)
        order = jax.random.permutation(key_order, NBD)
        return copies[order].astype(jnp.int32)
    return jax.vmap(one_group)(group_keys)


def setup_inputs(seed: int = 0) -> dict:
    seeds = jax.random.split(jax.random.key(seed), 3)
    return {
        "gradients": draw_gradients(jax.random.fold_in(seeds[2], 71), 0),
        "owners": draw_owners(jax.random.fold_in(seeds[2], 71), 0),
    }


def product(left_side, right_side):
    return jnp.dot(left_side, right_side, preferred_element_type=jnp.float32)

def inverse_root(factor):
    identity = jnp.eye(factor.shape[0], dtype=jnp.float32)
    factor_norm = jnp.sqrt(jnp.sum(factor * factor) + 1e-06)
    scaled = factor / factor_norm
    scaled_low = scaled.astype(jnp.bfloat16)
    first_step = ((5.0 * identity - scaled) * 0.25).astype(jnp.bfloat16)
    step_square = product(first_step, first_step).astype(jnp.bfloat16)
    partial_term = product(step_square, scaled_low).astype(jnp.bfloat16)
    next_scaled = product(step_square, partial_term)
    second_step = ((5.0 * identity - next_scaled) * 0.25).astype(jnp.bfloat16)
    return product(first_step, second_step).astype(jnp.bfloat16)

def precondition(block):
    block_low = block.astype(jnp.bfloat16)
    left_factor = product(block_low, block_low.T)
    right_factor = product(block_low.T, block_low)
    root_left = inverse_root(left_factor)
    root_right = inverse_root(right_factor)
    half_applied = product(root_left, block_low).astype(jnp.bfloat16)
    direction = product(half_applied, root_right)
    grad_norm = jnp.sqrt(jnp.sum(block * block))
    direction_norm = jnp.sqrt(jnp.sum(direction * direction) + 1e-06)
    graft_scale = grad_norm / direction_norm
    return ((graft_scale * direction).astype(jnp.bfloat16), graft_scale)

def slot_selector(owner_rows, owner_count):
    devices = jnp.arange(owner_count, dtype=jnp.int32)
    owned_by = (owner_rows[..., :, None] == devices).astype(jnp.int32)
    earlier = jnp.cumsum(owned_by, axis=-2) - owned_by
    slot_index = lax.optimization_barrier(jnp.sum(earlier * owned_by, axis=-1))
    slots = jnp.arange(MOST, dtype=jnp.int32)
    selector = (owner_rows[..., None, None, :] == devices[:, None, None]) & (slot_index[..., None, None, :] == slots[None, :, None])
    return selector.astype(jnp.float32)

def reference(gradients, owners):
    summed = gradients[0].astype(jnp.float32)
    for replica in range(1, N_DP):
        summed = summed + gradients[replica].astype(jnp.float32)
    blocks = jnp.transpose(summed, (1, 0, 2))
    updates, scales = lax.map(precondition, blocks)
    update_out = jnp.transpose(updates, (1, 0, 2))
    selector = slot_selector(owners, N_FSDP)
    group_scales = scales.reshape(N_DP, NBD)
    owner_scales = lax.optimization_barrier(jnp.sum(selector * group_scales[:, None, None, :], axis=3))
    return (update_out, owner_scales)
```

```python
import functools

import jax
import jax.numpy as jnp
from jax import lax
from jax.experimental import pallas as pl
from jax.experimental.pallas import tpu as pltpu
from jax.sharding import PartitionSpec as P

MOST = 2
PARTS = 4
SUBS = 2 * PARTS
SLOTS = 4
STARTS = (8, 12, 12, 12)
PERIODS = 16
LANE = 128
LINES = 8
FAR_FIRST = (4, -3, 3, -2, 2, -1, 1, 0)
ACROSS = 4
CORES = 2
MESH = pl.DeviceIdType.MESH


def product(left_side, right_side):
    return jnp.dot(left_side, right_side, preferred_element_type=jnp.float32)


def fives(size):
    shape = (size, size)
    down = lax.broadcasted_iota(jnp.int32, shape, 0)
    across = lax.broadcasted_iota(jnp.int32, shape, 1)
    return jnp.where(down == across, 5.0, 0.0)


def within(index, count):
    return jnp.where(index >= count, index - count, index)


def wave_of(device):
    core = lax.rem(device, CORES)
    chip = lax.div(device, CORES)
    column, row = lax.rem(chip, ACROSS), lax.div(chip, ACROSS)
    return CORES * core + lax.rem(column + row, 2), row * (ACROSS // 2) + lax.div(column, 2)


def each_receiver(part, device, batch, send):
    core, parity = lax.div(part, CORES), lax.rem(part, CORES)
    chip = lax.div(device, CORES)
    first, mine = lax.div(lax.rem(chip, ACROSS), 2), lax.div(chip, ACROSS)
    even = lax.rem(parity + mine, 2)
    for offset in FAR_FIRST[2 * batch : 2 * batch + 2]:
        row = within(mine + offset % LINES, LINES)
        odd = 1 - even if offset % 2 else even
        for pair in (first, 1 - first):
            column = 2 * pair + odd
            send(row * (ACROSS // 2) + pair, (row * ACROSS + column) * CORES + core)


def blocks_stepped(index):
    lane, row = index >> 3, index & 7
    core, column = lane & 1, lane >> 1
    wave = 2 * core + ((column + row) & 1)
    return wave * 16 + row * 2 + (column >> 1)


def step_kernel(
    planes, count, x_ref, owners_ref, out_ref, slots_ref,
    own, come, turned, ready, gathered, back, returned, scale_mine, column_scales, scales, restored,
    block, scaled_low, first_step, step_square, partial_term, second_step, root, half_applied,
    grad_squares,
    load_sem, send_sem, recv_sem, push_sem, block_sem, row_sem, column_sem, scale_sem, plane_sem,
):
    plane = lax.axis_index("dp")
    me = lax.axis_index("fsdp")
    half = planes // 2
    group = count
    part_size = group // PARTS
    rows, width = out_ref.shape[0], out_ref.shape[2] // 2
    few = rows // 2
    lanes = ACROSS * CORES
    lines = count // lanes
    my_line, my_lane = lax.div(me, lanes), lax.rem(me, lanes)
    my_wave, my_place = wave_of(me)
    my_block = my_wave * part_size + my_place
    barrier = pltpu.get_barrier_semaphore()

    goals = [
        [within(plane + (far if way == 0 else planes - far), planes) for far in range(half + 1)]
        for way in (0, 1)
    ]

    def goal(way, far):
        return goals[way][far]

    def blocks(part):
        return pl.ds(pl.multiple_of(part * part_size, part_size), part_size)

    def place_of(sub):
        return pl.ds(lax.rem(sub, 2) * few, few), lax.div(sub, 2)

    def raw(way, far, sub):
        lines_of, part = place_of(sub)
        first = pl.multiple_of(goal(way, far) * group + part * part_size, part_size)
        return x_ref.at[0, lines_of, pl.ds(first, part_size), :]

    def slot(way, far):
        return 0 if far == 0 else far + way * (half - 1)

    def kept(way, far, sub):
        lines_of, part = place_of(sub)
        return own.at[slot(way, far), lines_of, blocks(part), :]

    def landed(way, far, sub):
        lines_of, part = place_of(sub)
        return come.at[way, far - 1, lines_of, blocks(part), :]

    def copy(way, far, sub, source):
        return pltpu.make_async_remote_copy(
            src_ref=source,
            dst_ref=landed(way, far, sub),
            send_sem=send_sem.at[way, far - 1, sub],
            recv_sem=recv_sem.at[way, far - 1, sub],
            device_id=(goal(way, 1), me),
            device_id_type=MESH,
        )

    def arrived(way, far, sub):
        copy(way, far, sub, landed(way, far, sub)).wait_recv()

    def load(way, far):
        first, size = (way * few, few) if far == half - 1 else (0, rows)
        start = pl.multiple_of(goal(way, far) * group, group)
        return pltpu.make_async_copy(
            x_ref.at[0, pl.ds(first, size), pl.ds(start, group), :],
            own.at[slot(way, far), pl.ds(first, size), :, :],
            load_sem.at[slot(way, far)],
        )

    def relay(way, far, sub):
        arrived(way, far + 1, sub)
        mine = kept(way, far, sub)
        total = mine[...].astype(jnp.float32) + landed(way, far + 1, sub)[...].astype(jnp.float32)
        mine[...] = total.astype(jnp.bfloat16)
        copy(way, far, sub, mine).start()

    def first_relay(sub):
        far = half - 1
        for way in (0, 1):

            @pl.when(lax.rem(sub, 2) != way)
            def _():
                copy(way, far, sub, raw(way, far, sub)).start()
                relay(1 - way, far, sub)

    def push(source, target, other, sent, got):
        pltpu.make_async_remote_copy(
            src_ref=source,
            dst_ref=target,
            send_sem=sent,
            recv_sem=got,
            device_id=(plane, other),
            device_id_type=MESH,
        ).start()

    def settle(buffer, semaphore):
        pltpu.make_async_copy(buffer, buffer, semaphore).wait()

    def in_column(step):
        return within(me + step * lanes, count)

    def in_row(step):
        return my_line * lanes + within(my_lane + step, lanes)

    def finish(sub):
        arrived(0, 1, sub)
        arrived(1, 1, sub)
        total = kept(0, 0, sub)[...].astype(jnp.float32)
        total += landed(0, 1, sub)[...].astype(jnp.float32)
        total += landed(1, 1, sub)[...].astype(jnp.float32)
        flat = total.reshape(few * part_size, 2 * width)
        tiles = [turned.at[tile] for tile in range(2 * width // LANE)]
        start = pl.multiple_of(lax.rem(sub, 2) * (few * part_size), few * part_size)
        for tile, lane in enumerate(tiles):
            lane[pl.ds(start, few * part_size), :] = flat[:, tile * LANE : (tile + 1) * LANE]

        @pl.when(lax.rem(sub, 2) == 1)
        def _():
            part = lax.div(sub, 2)
            for index in range(part_size):
                pieces = [lane[pl.ds(index, rows, stride=part_size), :] for lane in tiles]
                message = [
                    jnp.concatenate(pieces[: len(pieces) // 2], axis=1),
                    jnp.concatenate(pieces[len(pieces) // 2 :], axis=1),
                ]
                ready[part * part_size + index] = jnp.concatenate(message, axis=0).astype(
                    jnp.bfloat16
                )

    def hand_out(part, batch):
        def send(place, other):
            source = ready.at[part * part_size + place]

            @pl.when(other != me)
            def _():
                push(source, gathered.at[me], other, push_sem.at[0], block_sem)

            @pl.when(other == me)
            def _():
                pltpu.make_async_copy(source, gathered.at[me], block_sem).start()

        each_receiver(part, me, batch, send)

    size = count * rows

    def take_block():
        settle(gathered, block_sem)
        received = gathered[...].astype(jnp.float32)
        sides = [received[:, :rows, :], received[:, rows:, :]]
        whole = jnp.concatenate([side.reshape(size, width) for side in sides], axis=1)
        grad_squares[...] = jnp.broadcast_to(
            jnp.sum(whole * whole, keepdims=True), grad_squares.shape
        )
        block[...] = whole.astype(jnp.bfloat16)

    def take_factor():
        factor = lax.dot_general(
            block[...], block[...], (((1,), (1,)), ((), ())), preferred_element_type=jnp.float32
        )
        scaled = factor * (1.0 / jnp.sqrt(jnp.sum(factor * factor, keepdims=True) + 1e-06))
        scaled_low[...] = scaled.astype(jnp.bfloat16)
        first_step[...] = ((fives(size) - scaled) * 0.25).astype(jnp.bfloat16)

    def take_square():
        step_square[...] = product(first_step[...], first_step[...]).astype(jnp.bfloat16)

    def take_partial():
        partial_term[...] = product(step_square[...], scaled_low[...]).astype(jnp.bfloat16)

    def take_second():
        next_scaled = product(step_square[...], partial_term[...])
        second_step[...] = ((fives(size) - next_scaled) * 0.25).astype(jnp.bfloat16)

    def take_root():
        root[...] = product(first_step[...], second_step[...]).astype(jnp.bfloat16)

    def take_half():
        half_applied[...] = product(root[...], block[...]).astype(jnp.bfloat16)

    def take_direction():
        direction = product(root[...], half_applied[...])
        graft = jnp.sqrt(grad_squares[...][:, :1]) / jnp.sqrt(
            jnp.sum(direction * direction, keepdims=True) + 1e-06
        )
        update = direction * graft
        sides = [update[:, :width], update[:, width:]]
        back[...] = jnp.concatenate(
            [side.reshape(count, rows, width) for side in sides], axis=1
        ).astype(jnp.bfloat16)
        scale_mine[...] = jnp.broadcast_to(graft, scale_mine.shape)

    def give_scale():
        def line(step, carry):
            push(scale_mine, column_scales.at[my_line], in_column(step), push_sem.at[2], column_sem)
            return carry

        lax.fori_loop(1, lines, line, 0)
        pltpu.make_async_copy(scale_mine, column_scales.at[my_line], column_sem).start()
        pltpu.make_async_copy(back.at[me], returned.at[my_block], row_sem.at[my_wave]).start()

    def give_rows(quarter):
        def to_lane(step, carry):
            lane = within(my_lane + step, lanes)
            for offset in FAR_FIRST:
                other = within(my_line + offset % lines, lines) * lanes + lane

                @pl.when(other != me)
                def _():
                    push(
                        back.at[other], returned.at[my_block], other,
                        push_sem.at[1], row_sem.at[my_wave],
                    )

            return carry

        lax.fori_loop(quarter * lanes // 4, (quarter + 1) * lanes // 4, to_lane, 0)

    def first_rows():
        give_scale()
        give_rows(0)

    stages = [
        take_block, take_factor, take_square, take_partial, take_second, take_root, take_half,
        take_direction, first_rows, *[functools.partial(give_rows, q) for q in (1, 2, 3)],
    ]

    loads = [load(way, far) for far in range(half - 1, 0, -1) for way in (0, 1)] + [load(0, 0)]
    for each in loads:
        each.start()
    def signal(semaphore, device):
        pl.semaphore_signal(semaphore, inc=1, device_id=device, device_id_type=MESH)

    def greet_column(step, carry):
        signal(barrier, (plane, in_column(step)))
        return carry

    def greet_row(step, carry):
        signal(barrier, (plane, in_row(step)))
        return carry

    def vouch(step, carry):
        signal(plane_sem, (plane, in_row(step)))
        return carry

    signal(barrier, (goal(0, 1), me))
    signal(barrier, (goal(1, 1), me))
    lax.fori_loop(1, lines, greet_column, 0)
    lax.fori_loop(1, lanes, greet_row, 0)
    pl.semaphore_wait(barrier, lines + lanes)

    def start_half_way(pair, carry):
        for way in (0, 1):
            sub = 2 * pair + way
            copy(way, half, sub, raw(way, half, sub)).start()
        return carry

    lax.fori_loop(0, SUBS // 2, start_half_way, 0)
    lax.fori_loop(1, lanes, vouch, 0)
    for each in loads:
        each.wait()
    first_relay(0)
    pl.semaphore_wait(plane_sem, lanes - 1)
    begin = STARTS[-1]
    for wave in reversed(range(PARTS - 1)):
        begin = jnp.where(my_wave == wave, STARTS[wave], begin)

    def period(now, carry):
        for turn in range(SLOTS):
            far = SLOTS - 1 - turn
            if far < half:
                lag = 2 * (half - far) - 3 if far else 2 * (half - 2)
                sub = now - lag

                @pl.when((sub >= 0) & (sub < SUBS))
                def _():
                    if far == half - 1:
                        first_relay(sub)
                    elif far > 0:
                        relay(0, far, sub)
                        relay(1, far, sub)
                    else:
                        finish(sub)

            lag = 2 * (half - 2) + (0 if turn == SLOTS - 1 else 1)
            last = now - lag

            @pl.when((last >= 0) & (last < SUBS) & (lax.rem(last + SUBS, 2) == 1))
            def _():
                hand_out(lax.div(last, 2), (turn + 1) % SLOTS)

            for number, stage in enumerate(stages):
                if (number + SLOTS - 1) % SLOTS == turn:
                    pl.when(now == begin + (number + SLOTS - 1) // SLOTS)(stage)
        return carry

    lax.fori_loop(0, PERIODS, period, 0)

    settle(column_scales, column_sem)
    mine_there = scales.at[pl.ds(my_lane * lines, lines)]

    def spread(step, carry):
        push(column_scales, mine_there, in_row(step), push_sem.at[3], scale_sem)
        return carry

    lax.fori_loop(1, lanes, spread, 0)
    pltpu.make_async_copy(column_scales, mine_there, scale_sem).start()

    def sent(pair, carry):
        for way in (0, 1):
            copy(way, half, 2 * pair + way, landed(way, half, 2 * pair + way)).wait_send()
            for far in range(1, half):
                for sub in (2 * pair, 2 * pair + 1):
                    copy(way, far, sub, landed(way, far, sub)).wait_send()
        return carry

    lax.fori_loop(0, SUBS // 2, sent, 0)
    settle(ready.at[pl.ds(0, count - 1)], push_sem.at[0])
    def restore(part, carry):
        settle(returned.at[blocks(part)], row_sem.at[part])
        flat = returned[blocks(part)].astype(jnp.float32).reshape(part_size * 2 * rows, width)
        for tile in range(width // LANE):
            lane = restored.at[tile]
            lane[...] = flat[:, tile * LANE : (tile + 1) * LANE]
            for side in range(2):
                first = side * width + tile * LANE
                for row in range(rows):
                    column = lane[pl.ds(side * rows + row, part_size, stride=2 * rows), :]
                    out_ref[row, blocks(part), first : first + LANE] = column.astype(jnp.bfloat16)
        return carry

    lax.fori_loop(0, PARTS - 1, restore, 0)
    settle(scales, scale_sem)
    factors = scales[...][:, 0, :1]
    square = (count, count)
    mine = jnp.broadcast_to((owners_ref[...] == me).astype(jnp.float32), square)
    stepped = blocks_stepped(lax.broadcasted_iota(jnp.int32, square, 0))
    across = lax.broadcasted_iota(jnp.int32, square, 1)
    owned = jnp.sum(jnp.where(across == stepped, mine, 0.0), axis=1, keepdims=True)
    earlier = jnp.sum(jnp.where(across < stepped, mine, 0.0), axis=1, keepdims=True)
    place = lax.broadcasted_iota(jnp.int32, (count, MOST), 1).astype(jnp.float32)
    picked = jnp.where((earlier == place) & (owned > 0.5), factors, 0.0)
    slots_ref[0] = jnp.sum(picked, axis=0, keepdims=True)
    restore(PARTS - 1, 0)

    settle(back.at[pl.ds(0, count - 1)], push_sem.at[1])
    settle(column_scales.at[pl.ds(0, lines - 1)], push_sem.at[2])
    settle(scales.at[pl.ds(0, (lanes - 1) * lines)], push_sem.at[3])


def on_device(gradients, owners):
    planes, count = lax.axis_size("dp"), lax.axis_size("fsdp")
    _, rows, blocks, width = gradients.shape
    group = blocks // planes
    half = planes // 2
    part_size = group // PARTS
    lines = count // (ACROSS * CORES)
    message = (group, 2 * rows, width // 2)
    matrix = (count * rows, count * rows)
    vmem = pl.BlockSpec(memory_space=pltpu.VMEM)
    return pl.pallas_call(
        functools.partial(step_kernel, planes, count),
        out_shape=(
            jax.ShapeDtypeStruct((rows, group, width), jnp.bfloat16),
            jax.ShapeDtypeStruct((1, 1, MOST), jnp.float32),
        ),
        in_specs=[pl.BlockSpec(memory_space=pltpu.HBM), vmem],
        out_specs=(vmem, vmem),
        scratch_shapes=[
            pltpu.VMEM((2 * half - 1, rows, group, width), jnp.bfloat16),
            pltpu.VMEM((2, half, rows, group, width), jnp.bfloat16),
            pltpu.VMEM((width // LANE, rows * part_size, LANE), jnp.float32),
            *[pltpu.VMEM(message, jnp.bfloat16)] * 4,
            pltpu.VMEM((1, 128), jnp.float32),
            pltpu.VMEM((lines, 1, 128), jnp.float32),
            pltpu.VMEM((count, 1, 128), jnp.float32),
            pltpu.VMEM((width // 2 // LANE, part_size * 2 * rows, LANE), jnp.float32),
            pltpu.VMEM((count * rows, width), jnp.bfloat16),
            *[pltpu.VMEM(matrix, jnp.bfloat16)] * 6,
            pltpu.VMEM((count * rows, width), jnp.bfloat16),
            pltpu.VMEM((1, 128), jnp.float32),
            pltpu.SemaphoreType.DMA((2 * half - 1,)),
            pltpu.SemaphoreType.DMA((2, half, SUBS)),
            pltpu.SemaphoreType.DMA((2, half, SUBS)),
            pltpu.SemaphoreType.DMA((4,)),
            pltpu.SemaphoreType.DMA,
            pltpu.SemaphoreType.DMA((PARTS,)),
            pltpu.SemaphoreType.DMA,
            pltpu.SemaphoreType.DMA,
            pltpu.SemaphoreType.REGULAR,
        ],
        compiler_params=pltpu.CompilerParams(
            collective_id=0, has_side_effects=True, vmem_limit_bytes=53 * 2**20
        ),
    )(gradients, owners)


def solution(mesh):
    placed = (P("dp", "fsdp", None, None), P("dp", None))
    return jax.shard_map(
        on_device,
        mesh=mesh,
        in_specs=placed,
        out_specs=(P("fsdp", "dp", None), P("dp", "fsdp", None)),
        check_vma=False,
    )
```

```python
import functools

import jax
import jax.numpy as jnp
from jax import lax
from jax.experimental import pallas as pl
from jax.experimental.pallas import tpu as pltpu
from jax.sharding import PartitionSpec as P

MOST = 2
PARTS = 4
SUBS = 2 * PARTS
SLOTS = 4
STARTS = (8, 12, 12, 12)
PERIODS = 16
LANE = 128
LINES = 8
FAR_FIRST = (4, -3, 3, -2, 2, -1, 1, 0)
ACROSS = 4
CORES = 2
MESH = pl.DeviceIdType.MESH


def product(left_side, right_side):
    return jnp.dot(left_side, right_side, preferred_element_type=jnp.float32)


def fives(size):
    shape = (size, size)
    down = lax.broadcasted_iota(jnp.int32, shape, 0)
    across = lax.broadcasted_iota(jnp.int32, shape, 1)
    return jnp.where(down == across, 5.0, 0.0)


def within(index, count):
    return jnp.where(index >= count, index - count, index)


def wave_of(device):
    core = lax.rem(device, CORES)
    chip = lax.div(device, CORES)
    column, row = lax.rem(chip, ACROSS), lax.div(chip, ACROSS)
    return CORES * core + lax.rem(column + row, 2), row * (ACROSS // 2) + lax.div(column, 2)


def each_receiver(part, device, batch, send):
    core, parity = lax.div(part, CORES), lax.rem(part, CORES)
    chip = lax.div(device, CORES)
    first, mine = lax.div(lax.rem(chip, ACROSS), 2), lax.div(chip, ACROSS)
    even = lax.rem(parity + mine, 2)
    for offset in FAR_FIRST[2 * batch : 2 * batch + 2]:
        row = within(mine + offset % LINES, LINES)
        odd = 1 - even if offset % 2 else even
        for pair in (first, 1 - first):
            column = 2 * pair + odd
            send(row * (ACROSS // 2) + pair, (row * ACROSS + column) * CORES + core, offset == 0)


def blocks_stepped(index):
    lane, row = index >> 3, index & 7
    core, column = lane & 1, lane >> 1
    wave = 2 * core + ((column + row) & 1)
    return wave * 16 + row * 2 + (column >> 1)


def step_kernel(
    planes, count, x_ref, owners_ref, out_ref, slots_ref,
    own, come, turned, ready, gathered, back, returned, scale_mine, column_scales, scales, restored,
    block, scaled_low, first_step, step_square, partial_term, second_step, root, half_applied,
    grad_squares,
    load_sem, send_sem, recv_sem, push_sem, block_sem, row_sem, column_sem, scale_sem, plane_sem,
):
    plane = lax.axis_index("dp")
    me = lax.axis_index("fsdp")
    half = planes // 2
    group = count
    part_size = group // PARTS
    rows, width = out_ref.shape[0], out_ref.shape[2] // 2
    few = rows // 2
    lanes = ACROSS * CORES
    lines = count // lanes
    my_line, my_lane = lax.div(me, lanes), lax.rem(me, lanes)
    my_wave, my_place = wave_of(me)
    my_block = my_wave * part_size + my_place
    barrier = pltpu.get_barrier_semaphore()

    goals = [
        [within(plane + (far if way == 0 else planes - far), planes) for far in range(half + 1)]
        for way in (0, 1)
    ]

    def goal(way, far):
        return goals[way][far]

    def blocks(part):
        return pl.ds(pl.multiple_of(part * part_size, part_size), part_size)

    def place_of(sub):
        return pl.ds(lax.rem(sub, 2) * few, few), lax.div(sub, 2)

    def raw(way, far, sub):
        lines_of, part = place_of(sub)
        first = pl.multiple_of(goal(way, far) * group + part * part_size, part_size)
        return x_ref.at[0, lines_of, pl.ds(first, part_size), :]

    def slot(way, far):
        return 0 if far == 0 else far + way * (half - 1)

    def kept(way, far, sub):
        lines_of, part = place_of(sub)
        return own.at[slot(way, far), lines_of, blocks(part), :]

    def landed(way, far, sub):
        lines_of, part = place_of(sub)
        return come.at[way, far - 1, lines_of, blocks(part), :]

    def copy(way, far, sub, source):
        return pltpu.make_async_remote_copy(
            src_ref=source,
            dst_ref=landed(way, far, sub),
            send_sem=send_sem.at[way, far - 1, sub],
            recv_sem=recv_sem.at[way, far - 1, sub],
            device_id=(goal(way, 1), me),
            device_id_type=MESH,
        )

    def arrived(way, far, sub):
        copy(way, far, sub, landed(way, far, sub)).wait_recv()

    def load(way, far):
        first, size = (way * few, few) if far == half - 1 else (0, rows)
        start = pl.multiple_of(goal(way, far) * group, group)
        return pltpu.make_async_copy(
            x_ref.at[0, pl.ds(first, size), pl.ds(start, group), :],
            own.at[slot(way, far), pl.ds(first, size), :, :],
            load_sem.at[slot(way, far)],
        )

    def relay(way, far, sub):
        arrived(way, far + 1, sub)
        mine = kept(way, far, sub)
        total = mine[...].astype(jnp.float32) + landed(way, far + 1, sub)[...].astype(jnp.float32)
        mine[...] = total.astype(jnp.bfloat16)
        copy(way, far, sub, mine).start()

    def first_relay(sub):
        far = half - 1
        for way in (0, 1):

            @pl.when(lax.rem(sub, 2) != way)
            def _():
                copy(way, far, sub, raw(way, far, sub)).start()
                relay(1 - way, far, sub)

    def push(source, target, other, sent, got):
        pltpu.make_async_remote_copy(
            src_ref=source,
            dst_ref=target,
            send_sem=sent,
            recv_sem=got,
            device_id=(plane, other),
            device_id_type=MESH,
        ).start()

    def settle(buffer, semaphore):
        pltpu.make_async_copy(buffer, buffer, semaphore).wait()

    def in_column(step):
        return within(me + step * lanes, count)

    def in_row(step):
        return my_line * lanes + within(my_lane + step, lanes)

    def finish(sub):
        arrived(0, 1, sub)
        arrived(1, 1, sub)
        total = kept(0, 0, sub)[...].astype(jnp.float32)
        total += landed(0, 1, sub)[...].astype(jnp.float32)
        total += landed(1, 1, sub)[...].astype(jnp.float32)
        flat = total.reshape(few * part_size, 2 * width)
        tiles = [turned.at[tile] for tile in range(2 * width // LANE)]
        start = pl.multiple_of(lax.rem(sub, 2) * (few * part_size), few * part_size)
        for tile, lane in enumerate(tiles):
            lane[pl.ds(start, few * part_size), :] = flat[:, tile * LANE : (tile + 1) * LANE]

        @pl.when(lax.rem(sub, 2) == 1)
        def _():
            part = lax.div(sub, 2)
            for index in range(part_size):
                pieces = [lane[pl.ds(index, rows, stride=part_size), :] for lane in tiles]
                message = [
                    jnp.concatenate(pieces[: len(pieces) // 2], axis=1),
                    jnp.concatenate(pieces[len(pieces) // 2 :], axis=1),
                ]
                ready[part * part_size + index] = jnp.concatenate(message, axis=0).astype(
                    jnp.bfloat16
                )

    def hand_out(part, batch):
        def send(place, other, own_row):
            source = ready.at[part * part_size + place]

            def over():
                push(source, gathered.at[me], other, push_sem.at[0], block_sem)

            if not own_row:
                over()
                return
            pl.when(other != me)(over)

            @pl.when(other == me)
            def _():
                pltpu.make_async_copy(source, gathered.at[me], block_sem).start()

        each_receiver(part, me, batch, send)

    size = count * rows

    def take_block():
        settle(gathered, block_sem)
        received = gathered[...].astype(jnp.float32)
        sides = [received[:, :rows, :], received[:, rows:, :]]
        whole = jnp.concatenate([side.reshape(size, width) for side in sides], axis=1)
        grad_squares[...] = jnp.broadcast_to(
            jnp.sum(whole * whole, keepdims=True), grad_squares.shape
        )
        block[...] = whole.astype(jnp.bfloat16)

    def take_factor():
        factor = lax.dot_general(
            block[...], block[...], (((1,), (1,)), ((), ())), preferred_element_type=jnp.float32
        )
        scaled = factor * (1.0 / jnp.sqrt(jnp.sum(factor * factor, keepdims=True) + 1e-06))
        scaled_low[...] = scaled.astype(jnp.bfloat16)
        first_step[...] = ((fives(size) - scaled) * 0.25).astype(jnp.bfloat16)

    def take_square():
        step_square[...] = product(first_step[...], first_step[...]).astype(jnp.bfloat16)

    def take_partial():
        partial_term[...] = product(step_square[...], scaled_low[...]).astype(jnp.bfloat16)

    def take_second():
        next_scaled = product(step_square[...], partial_term[...])
        second_step[...] = ((fives(size) - next_scaled) * 0.25).astype(jnp.bfloat16)

    def take_root():
        root[...] = product(first_step[...], second_step[...]).astype(jnp.bfloat16)

    def take_half():
        half_applied[...] = product(root[...], block[...]).astype(jnp.bfloat16)

    def take_direction():
        direction = product(root[...], half_applied[...])
        graft = jnp.sqrt(grad_squares[...][:, :1]) / jnp.sqrt(
            jnp.sum(direction * direction, keepdims=True) + 1e-06
        )
        update = direction * graft
        sides = [update[:, :width], update[:, width:]]
        back[...] = jnp.concatenate(
            [side.reshape(count, rows, width) for side in sides], axis=1
        ).astype(jnp.bfloat16)
        scale_mine[...] = jnp.broadcast_to(graft, scale_mine.shape)

    def give_scale():
        def line(step, carry):
            push(scale_mine, column_scales.at[my_line], in_column(step), push_sem.at[2], column_sem)
            return carry

        lax.fori_loop(1, lines, line, 0)
        pltpu.make_async_copy(scale_mine, column_scales.at[my_line], column_sem).start()
        pltpu.make_async_copy(back.at[me], returned.at[my_block], row_sem.at[my_wave]).start()

    def give_rows(quarter):
        for step in range(quarter * lanes // 4, (quarter + 1) * lanes // 4):
            lane = within(my_lane + step, lanes)
            for offset in FAR_FIRST:
                if step or offset:
                    other = within(my_line + offset % lines, lines) * lanes + lane
                    push(
                        back.at[other], returned.at[my_block], other,
                        push_sem.at[1], row_sem.at[my_wave],
                    )

    def first_rows():
        give_scale()
        give_rows(0)

    stages = [
        take_block, take_factor, take_square, take_partial, take_second, take_root, take_half,
        take_direction, first_rows, *[functools.partial(give_rows, q) for q in (1, 2, 3)],
    ]

    loads = [load(way, far) for far in range(half - 1, 0, -1) for way in (0, 1)] + [load(0, 0)]
    for each in loads:
        each.start()
    def signal(semaphore, device):
        pl.semaphore_signal(semaphore, inc=1, device_id=device, device_id_type=MESH)

    def greet_column(step, carry):
        signal(barrier, (plane, in_column(step)))
        return carry

    def greet_row(step, carry):
        signal(barrier, (plane, in_row(step)))
        return carry

    def vouch(step, carry):
        signal(plane_sem, (plane, in_row(step)))
        return carry

    signal(barrier, (goal(0, 1), me))
    signal(barrier, (goal(1, 1), me))
    lax.fori_loop(1, lines, greet_column, 0)
    lax.fori_loop(1, lanes, greet_row, 0)
    pl.semaphore_wait(barrier, lines + lanes)

    def start_half_way(pair, carry):
        for way in (0, 1):
            sub = 2 * pair + way
            copy(way, half, sub, raw(way, half, sub)).start()
        return carry

    lax.fori_loop(0, SUBS // 2, start_half_way, 0)
    lax.fori_loop(1, lanes, vouch, 0)
    for each in loads:
        each.wait()
    first_relay(0)
    pl.semaphore_wait(plane_sem, lanes - 1)
    begin = STARTS[-1]
    for wave in reversed(range(PARTS - 1)):
        begin = jnp.where(my_wave == wave, STARTS[wave], begin)

    def period(now, carry):
        for turn in range(SLOTS):
            far = SLOTS - 1 - turn
            if far < half:
                lag = 2 * (half - far) - 3 if far else 2 * (half - 2)
                sub = now - lag

                @pl.when((sub >= 0) & (sub < SUBS))
                def _():
                    if far == half - 1:
                        first_relay(sub)
                    elif far > 0:
                        relay(0, far, sub)
                        relay(1, far, sub)
                    else:
                        finish(sub)

            lag = 2 * (half - 2) + (0 if turn == SLOTS - 1 else 1)
            last = now - lag

            @pl.when((last >= 0) & (last < SUBS) & (lax.rem(last + SUBS, 2) == 1))
            def _():
                hand_out(lax.div(last, 2), (turn + 1) % SLOTS)

            for number, stage in enumerate(stages):
                if (number + SLOTS - 1) % SLOTS == turn:
                    pl.when(now == begin + (number + SLOTS - 1) // SLOTS)(stage)
        return carry

    lax.fori_loop(0, PERIODS, period, 0)

    settle(column_scales, column_sem)
    mine_there = scales.at[pl.ds(my_lane * lines, lines)]

    def spread(step, carry):
        push(column_scales, mine_there, in_row(step), push_sem.at[3], scale_sem)
        return carry

    lax.fori_loop(1, lanes, spread, 0)
    pltpu.make_async_copy(column_scales, mine_there, scale_sem).start()

    def sent(pair, carry):
        for way in (0, 1):
            copy(way, half, 2 * pair + way, landed(way, half, 2 * pair + way)).wait_send()
            for far in range(1, half):
                for sub in (2 * pair, 2 * pair + 1):
                    copy(way, far, sub, landed(way, far, sub)).wait_send()
        return carry

    lax.fori_loop(0, SUBS // 2, sent, 0)
    settle(ready.at[pl.ds(0, count - 1)], push_sem.at[0])
    def restore(part, carry):
        settle(returned.at[blocks(part)], row_sem.at[part])
        flat = returned[blocks(part)].astype(jnp.float32).reshape(part_size * 2 * rows, width)
        for tile in range(width // LANE):
            lane = restored.at[tile]
            lane[...] = flat[:, tile * LANE : (tile + 1) * LANE]
            for side in range(2):
                first = side * width + tile * LANE
                for row in range(rows):
                    column = lane[pl.ds(side * rows + row, part_size, stride=2 * rows), :]
                    out_ref[row, blocks(part), first : first + LANE] = column.astype(jnp.bfloat16)
        return carry

    lax.fori_loop(0, PARTS - 1, restore, 0)
    settle(scales, scale_sem)
    factors = scales[...][:, 0, :1]
    square = (count, count)
    mine = jnp.broadcast_to((owners_ref[...] == me).astype(jnp.float32), square)
    stepped = blocks_stepped(lax.broadcasted_iota(jnp.int32, square, 0))
    across = lax.broadcasted_iota(jnp.int32, square, 1)
    owned = jnp.sum(jnp.where(across == stepped, mine, 0.0), axis=1, keepdims=True)
    earlier = jnp.sum(jnp.where(across < stepped, mine, 0.0), axis=1, keepdims=True)
    place = lax.broadcasted_iota(jnp.int32, (count, MOST), 1).astype(jnp.float32)
    picked = jnp.where((earlier == place) & (owned > 0.5), factors, 0.0)
    slots_ref[0] = jnp.sum(picked, axis=0, keepdims=True)
    restore(PARTS - 1, 0)

    settle(back.at[pl.ds(0, count - 1)], push_sem.at[1])
    settle(column_scales.at[pl.ds(0, lines - 1)], push_sem.at[2])
    settle(scales.at[pl.ds(0, (lanes - 1) * lines)], push_sem.at[3])


def on_device(gradients, owners):
    planes, count = lax.axis_size("dp"), lax.axis_size("fsdp")
    _, rows, blocks, width = gradients.shape
    group = blocks // planes
    half = planes // 2
    part_size = group // PARTS
    lines = count // (ACROSS * CORES)
    message = (group, 2 * rows, width // 2)
    matrix = (count * rows, count * rows)
    vmem = pl.BlockSpec(memory_space=pltpu.VMEM)
    return pl.pallas_call(
        functools.partial(step_kernel, planes, count),
        out_shape=(
            jax.ShapeDtypeStruct((rows, group, width), jnp.bfloat16),
            jax.ShapeDtypeStruct((1, 1, MOST), jnp.float32),
        ),
        in_specs=[pl.BlockSpec(memory_space=pltpu.HBM), vmem],
        out_specs=(vmem, vmem),
        scratch_shapes=[
            pltpu.VMEM((2 * half - 1, rows, group, width), jnp.bfloat16),
            pltpu.VMEM((2, half, rows, group, width), jnp.bfloat16),
            pltpu.VMEM((width // LANE, rows * part_size, LANE), jnp.float32),
            *[pltpu.VMEM(message, jnp.bfloat16)] * 4,
            pltpu.VMEM((1, 128), jnp.float32),
            pltpu.VMEM((lines, 1, 128), jnp.float32),
            pltpu.VMEM((count, 1, 128), jnp.float32),
            pltpu.VMEM((width // 2 // LANE, part_size * 2 * rows, LANE), jnp.float32),
            pltpu.VMEM((count * rows, width), jnp.bfloat16),
            *[pltpu.VMEM(matrix, jnp.bfloat16)] * 6,
            pltpu.VMEM((count * rows, width), jnp.bfloat16),
            pltpu.VMEM((1, 128), jnp.float32),
            pltpu.SemaphoreType.DMA((2 * half - 1,)),
            pltpu.SemaphoreType.DMA((2, half, SUBS)),
            pltpu.SemaphoreType.DMA((2, half, SUBS)),
            pltpu.SemaphoreType.DMA((4,)),
            pltpu.SemaphoreType.DMA,
            pltpu.SemaphoreType.DMA((PARTS,)),
            pltpu.SemaphoreType.DMA,
            pltpu.SemaphoreType.DMA,
            pltpu.SemaphoreType.REGULAR,
        ],
        compiler_params=pltpu.CompilerParams(
            collective_id=0, has_side_effects=True, vmem_limit_bytes=53 * 2**20
        ),
    )(gradients, owners)


def solution(mesh):
    placed = (P("dp", "fsdp", None, None), P("dp", None))
    return jax.shard_map(
        on_device,
        mesh=mesh,
        in_specs=placed,
        out_specs=(P("fsdp", "dp", None), P("dp", "fsdp", None)),
        check_vma=False,
    )
```

```python
import functools

import jax
import jax.numpy as jnp
from jax import lax
from jax.experimental import pallas as pl
from jax.experimental.pallas import tpu as pltpu
from jax.sharding import PartitionSpec as P

MOST = 2
PARTS = 4
SUBS = 2 * PARTS
SLOTS = 4
PERIODS = 12
LANE = 128
LINES = 8
FAR_FIRST = (4, -3, 3, -2, 2, -1, 1, 0)
ACROSS = 4
CORES = 2
MESH = pl.DeviceIdType.MESH


def product(left_side, right_side):
    return jnp.dot(left_side, right_side, preferred_element_type=jnp.float32)


def fives(size):
    shape = (size, size)
    down = lax.broadcasted_iota(jnp.int32, shape, 0)
    across = lax.broadcasted_iota(jnp.int32, shape, 1)
    return jnp.where(down == across, 5.0, 0.0)


def within(index, count):
    return jnp.where(index >= count, index - count, index)


def wave_of(device):
    core = lax.rem(device, CORES)
    chip = lax.div(device, CORES)
    column, row = lax.rem(chip, ACROSS), lax.div(chip, ACROSS)
    return CORES * core + lax.rem(column + row, 2), row * (ACROSS // 2) + lax.div(column, 2)


def each_receiver(part, device, batch, send):
    core, parity = lax.div(part, CORES), lax.rem(part, CORES)
    chip = lax.div(device, CORES)
    first, mine = lax.div(lax.rem(chip, ACROSS), 2), lax.div(chip, ACROSS)
    even = lax.rem(parity + mine, 2)
    for offset in FAR_FIRST[2 * batch : 2 * batch + 2]:
        row = within(mine + offset % LINES, LINES)
        odd = 1 - even if offset % 2 else even
        for pair in (first, 1 - first):
            column = 2 * pair + odd
            send(row * (ACROSS // 2) + pair, (row * ACROSS + column) * CORES + core, offset == 0)


def blocks_stepped(index):
    lane, row = index >> 3, index & 7
    core, column = lane & 1, lane >> 1
    wave = 2 * core + ((column + row) & 1)
    return wave * 16 + row * 2 + (column >> 1)


def step_kernel(
    planes, count, x_ref, owners_ref, out_ref, slots_ref,
    own, come, turned, ready, gathered, back, returned, scale_mine, column_scales, scales, restored,
    block, scaled_low, first_step, step_square, partial_term, second_step, root, half_applied,
    grad_squares,
    load_sem, send_sem, recv_sem, push_sem, block_sem, row_sem, column_sem, scale_sem, plane_sem,
):
    plane = lax.axis_index("dp")
    me = lax.axis_index("fsdp")
    half = planes // 2
    group = count
    part_size = group // PARTS
    rows, width = out_ref.shape[0], out_ref.shape[2] // 2
    few = rows // 2
    lanes = ACROSS * CORES
    lines = count // lanes
    my_line, my_lane = lax.div(me, lanes), lax.rem(me, lanes)
    my_wave, my_place = wave_of(me)
    my_block = my_wave * part_size + my_place
    barrier = pltpu.get_barrier_semaphore()

    goals = [
        [within(plane + (far if way == 0 else planes - far), planes) for far in range(half + 1)]
        for way in (0, 1)
    ]

    def goal(way, far):
        return goals[way][far]

    def blocks(part):
        return pl.ds(pl.multiple_of(part * part_size, part_size), part_size)

    def place_of(sub):
        return pl.ds(lax.rem(sub, 2) * few, few), lax.div(sub, 2)

    def raw(way, far, sub):
        lines_of, part = place_of(sub)
        first = pl.multiple_of(goal(way, far) * group + part * part_size, part_size)
        return x_ref.at[0, lines_of, pl.ds(first, part_size), :]

    def slot(way, far):
        return 0 if far == 0 else far + way * (half - 1)

    def kept(way, far, sub):
        lines_of, part = place_of(sub)
        return own.at[slot(way, far), lines_of, blocks(part), :]

    def landed(way, far, sub):
        lines_of, part = place_of(sub)
        return come.at[way, far - 1, lines_of, blocks(part), :]

    def copy(way, far, sub, source):
        return pltpu.make_async_remote_copy(
            src_ref=source,
            dst_ref=landed(way, far, sub),
            send_sem=send_sem.at[way, far - 1, sub],
            recv_sem=recv_sem.at[way, far - 1, sub],
            device_id=(goal(way, 1), me),
            device_id_type=MESH,
        )

    def arrived(way, far, sub):
        copy(way, far, sub, landed(way, far, sub)).wait_recv()

    def load(way, far):
        first, size = (way * few, few) if far == half - 1 else (0, rows)
        start = pl.multiple_of(goal(way, far) * group, group)
        return pltpu.make_async_copy(
            x_ref.at[0, pl.ds(first, size), pl.ds(start, group), :],
            own.at[slot(way, far), pl.ds(first, size), :, :],
            load_sem.at[slot(way, far)],
        )

    def relay(way, far, sub):
        arrived(way, far + 1, sub)
        mine = kept(way, far, sub)
        total = mine[...].astype(jnp.float32) + landed(way, far + 1, sub)[...].astype(jnp.float32)
        mine[...] = total.astype(jnp.bfloat16)
        copy(way, far, sub, mine).start()

    def first_relay(sub):
        far = half - 1
        for way in (0, 1):

            @pl.when(lax.rem(sub, 2) != way)
            def _():
                copy(way, far, sub, raw(way, far, sub)).start()
                relay(1 - way, far, sub)

    def push(source, target, other, sent, got):
        pltpu.make_async_remote_copy(
            src_ref=source,
            dst_ref=target,
            send_sem=sent,
            recv_sem=got,
            device_id=(plane, other),
            device_id_type=MESH,
        ).start()

    def settle(buffer, semaphore):
        pltpu.make_async_copy(buffer, buffer, semaphore).wait()

    def in_column(step):
        return within(me + step * lanes, count)

    def in_row(step):
        return my_line * lanes + within(my_lane + step, lanes)

    def finish(sub):
        arrived(0, 1, sub)
        arrived(1, 1, sub)
        total = kept(0, 0, sub)[...].astype(jnp.float32)
        total += landed(0, 1, sub)[...].astype(jnp.float32)
        total += landed(1, 1, sub)[...].astype(jnp.float32)
        flat = total.reshape(few * part_size, 2 * width)
        tiles = [turned.at[tile] for tile in range(2 * width // LANE)]
        start = pl.multiple_of(lax.rem(sub, 2) * (few * part_size), few * part_size)
        for tile, lane in enumerate(tiles):
            lane[pl.ds(start, few * part_size), :] = flat[:, tile * LANE : (tile + 1) * LANE]

        @pl.when(lax.rem(sub, 2) == 1)
        def _():
            part = lax.div(sub, 2)
            for index in range(part_size):
                pieces = [lane[pl.ds(index, rows, stride=part_size), :] for lane in tiles]
                message = [
                    jnp.concatenate(pieces[: len(pieces) // 2], axis=1),
                    jnp.concatenate(pieces[len(pieces) // 2 :], axis=1),
                ]
                ready[part * part_size + index] = jnp.concatenate(message, axis=0).astype(
                    jnp.bfloat16
                )

    def hand_out(part, batch):
        def send(place, other, own_row):
            source = ready.at[part * part_size + place]

            def over():
                push(source, gathered.at[me], other, push_sem.at[0], block_sem)

            if not own_row:
                over()
                return
            pl.when(other != me)(over)

            @pl.when(other == me)
            def _():
                pltpu.make_async_copy(source, gathered.at[me], block_sem).start()

        each_receiver(part, me, batch, send)

    size = count * rows

    def take_block():
        settle(gathered, block_sem)
        received = gathered[...].astype(jnp.float32)
        sides = [received[:, :rows, :], received[:, rows:, :]]
        whole = jnp.concatenate([side.reshape(size, width) for side in sides], axis=1)
        grad_squares[...] = jnp.broadcast_to(
            jnp.sum(whole * whole, keepdims=True), grad_squares.shape
        )
        block[...] = whole.astype(jnp.bfloat16)

    def take_factor():
        factor = lax.dot_general(
            block[...], block[...], (((1,), (1,)), ((), ())), preferred_element_type=jnp.float32
        )
        scaled = factor * (1.0 / jnp.sqrt(jnp.sum(factor * factor, keepdims=True) + 1e-06))
        scaled_low[...] = scaled.astype(jnp.bfloat16)
        first_step[...] = ((fives(size) - scaled) * 0.25).astype(jnp.bfloat16)

    def take_square():
        step_square[...] = product(first_step[...], first_step[...]).astype(jnp.bfloat16)

    def take_partial():
        partial_term[...] = product(step_square[...], scaled_low[...]).astype(jnp.bfloat16)

    def take_second():
        next_scaled = product(step_square[...], partial_term[...])
        second_step[...] = ((fives(size) - next_scaled) * 0.25).astype(jnp.bfloat16)

    def take_root():
        root[...] = product(first_step[...], second_step[...]).astype(jnp.bfloat16)

    def take_half():
        half_applied[...] = product(root[...], block[...]).astype(jnp.bfloat16)

    def take_direction():
        direction = product(root[...], half_applied[...])
        graft = jnp.sqrt(grad_squares[...][:, :1]) / jnp.sqrt(
            jnp.sum(direction * direction, keepdims=True) + 1e-06
        )
        update = direction * graft
        sides = [update[:, :width], update[:, width:]]
        back[...] = jnp.concatenate(
            [side.reshape(count, rows, width) for side in sides], axis=1
        ).astype(jnp.bfloat16)
        scale_mine[...] = jnp.broadcast_to(graft, scale_mine.shape)

    def give_scale():
        def line(step, carry):
            push(scale_mine, column_scales.at[my_line], in_column(step), push_sem.at[2], column_sem)
            return carry

        lax.fori_loop(1, lines, line, 0)
        pltpu.make_async_copy(scale_mine, column_scales.at[my_line], column_sem).start()
        pltpu.make_async_copy(back.at[me], returned.at[my_block], row_sem.at[my_wave]).start()

    def give_rows(quarter):
        for step in range(quarter * lanes // 4, (quarter + 1) * lanes // 4):
            lane = within(my_lane + step, lanes)
            for offset in FAR_FIRST:
                if step or offset:
                    other = within(my_line + offset % lines, lines) * lanes + lane
                    push(
                        back.at[other], returned.at[my_block], other,
                        push_sem.at[1], row_sem.at[my_wave],
                    )

    def first_rows():
        give_scale()
        give_rows(0)

    stages = [
        take_block, take_factor, take_square, take_partial, take_second, take_root, take_half,
        take_direction, first_rows, *[functools.partial(give_rows, q) for q in (1, 2, 3)],
    ]

    loads = [load(way, far) for far in range(half - 1, 0, -1) for way in (0, 1)] + [load(0, 0)]
    for each in loads:
        each.start()
    def signal(semaphore, device):
        pl.semaphore_signal(semaphore, inc=1, device_id=device, device_id_type=MESH)

    def greet_column(step, carry):
        signal(barrier, (plane, in_column(step)))
        return carry

    def greet_row(step, carry):
        signal(barrier, (plane, in_row(step)))
        return carry

    def vouch(step, carry):
        signal(plane_sem, (plane, in_row(step)))
        return carry

    signal(barrier, (goal(0, 1), me))
    signal(barrier, (goal(1, 1), me))
    lax.fori_loop(1, lines, greet_column, 0)
    lax.fori_loop(1, lanes, greet_row, 0)
    pl.semaphore_wait(barrier, lines + lanes)

    def start_half_way(pair, carry):
        for way in (0, 1):
            sub = 2 * pair + way
            copy(way, half, sub, raw(way, half, sub)).start()
        return carry

    lax.fori_loop(0, SUBS // 2, start_half_way, 0)
    lax.fori_loop(1, lanes, vouch, 0)
    for each in loads:
        each.wait()
    first_relay(0)
    pl.semaphore_wait(plane_sem, lanes - 1)
    def period(now, carry):
        for turn in range(SLOTS):
            far = SLOTS - 1 - turn
            if far < half:
                lag = 2 * (half - far) - 3 if far else 2 * (half - 2)
                sub = now - lag

                @pl.when((sub >= 0) & (sub < SUBS))
                def _():
                    if far == half - 1:
                        first_relay(sub)
                    elif far > 0:
                        relay(0, far, sub)
                        relay(1, far, sub)
                    else:
                        finish(sub)

            lag = 2 * (half - 2) + (0 if turn == SLOTS - 1 else 1)
            last = now - lag

            @pl.when((last >= 0) & (last < SUBS - 1) & (lax.rem(last + SUBS, 2) == 1))
            def _():
                hand_out(lax.div(last, 2), (turn + 1) % SLOTS)

        return carry

    lax.fori_loop(0, PERIODS, period, 0)
    for batch in range(SLOTS):
        hand_out(PARTS - 1, batch)
    for stage in stages:
        stage()

    settle(column_scales, column_sem)
    mine_there = scales.at[pl.ds(my_lane * lines, lines)]

    def spread(step, carry):
        push(column_scales, mine_there, in_row(step), push_sem.at[3], scale_sem)
        return carry

    lax.fori_loop(1, lanes, spread, 0)
    pltpu.make_async_copy(column_scales, mine_there, scale_sem).start()

    def sent(pair, carry):
        for way in (0, 1):
            copy(way, half, 2 * pair + way, landed(way, half, 2 * pair + way)).wait_send()
            for far in range(1, half):
                for sub in (2 * pair, 2 * pair + 1):
                    copy(way, far, sub, landed(way, far, sub)).wait_send()
        return carry

    lax.fori_loop(0, SUBS // 2, sent, 0)
    settle(ready.at[pl.ds(0, count - 1)], push_sem.at[0])
    def restore(part, carry):
        settle(returned.at[blocks(part)], row_sem.at[part])
        flat = returned[blocks(part)].astype(jnp.float32).reshape(part_size * 2 * rows, width)
        for tile in range(width // LANE):
            lane = restored.at[tile]
            lane[...] = flat[:, tile * LANE : (tile + 1) * LANE]
            for side in range(2):
                first = side * width + tile * LANE
                for row in range(rows):
                    column = lane[pl.ds(side * rows + row, part_size, stride=2 * rows), :]
                    out_ref[row, blocks(part), first : first + LANE] = column.astype(jnp.bfloat16)
        return carry

    lax.fori_loop(0, PARTS - 1, restore, 0)
    settle(scales, scale_sem)
    factors = scales[...][:, 0, :1]
    square = (count, count)
    mine = jnp.broadcast_to((owners_ref[...] == me).astype(jnp.float32), square)
    stepped = blocks_stepped(lax.broadcasted_iota(jnp.int32, square, 0))
    across = lax.broadcasted_iota(jnp.int32, square, 1)
    owned = jnp.sum(jnp.where(across == stepped, mine, 0.0), axis=1, keepdims=True)
    earlier = jnp.sum(jnp.where(across < stepped, mine, 0.0), axis=1, keepdims=True)
    place = lax.broadcasted_iota(jnp.int32, (count, MOST), 1).astype(jnp.float32)
    picked = jnp.where((earlier == place) & (owned > 0.5), factors, 0.0)
    slots_ref[0] = jnp.sum(picked, axis=0, keepdims=True)
    restore(PARTS - 1, 0)

    settle(back.at[pl.ds(0, count - 1)], push_sem.at[1])
    settle(column_scales.at[pl.ds(0, lines - 1)], push_sem.at[2])
    settle(scales.at[pl.ds(0, (lanes - 1) * lines)], push_sem.at[3])


def on_device(gradients, owners):
    planes, count = lax.axis_size("dp"), lax.axis_size("fsdp")
    _, rows, blocks, width = gradients.shape
    group = blocks // planes
    half = planes // 2
    part_size = group // PARTS
    lines = count // (ACROSS * CORES)
    message = (group, 2 * rows, width // 2)
    matrix = (count * rows, count * rows)
    vmem = pl.BlockSpec(memory_space=pltpu.VMEM)
    return pl.pallas_call(
        functools.partial(step_kernel, planes, count),
        out_shape=(
            jax.ShapeDtypeStruct((rows, group, width), jnp.bfloat16),
            jax.ShapeDtypeStruct((1, 1, MOST), jnp.float32),
        ),
        in_specs=[pl.BlockSpec(memory_space=pltpu.HBM), vmem],
        out_specs=(vmem, vmem),
        scratch_shapes=[
            pltpu.VMEM((2 * half - 1, rows, group, width), jnp.bfloat16),
            pltpu.VMEM((2, half, rows, group, width), jnp.bfloat16),
            pltpu.VMEM((width // LANE, rows * part_size, LANE), jnp.float32),
            *[pltpu.VMEM(message, jnp.bfloat16)] * 4,
            pltpu.VMEM((1, 128), jnp.float32),
            pltpu.VMEM((lines, 1, 128), jnp.float32),
            pltpu.VMEM((count, 1, 128), jnp.float32),
            pltpu.VMEM((width // 2 // LANE, part_size * 2 * rows, LANE), jnp.float32),
            pltpu.VMEM((count * rows, width), jnp.bfloat16),
            *[pltpu.VMEM(matrix, jnp.bfloat16)] * 6,
            pltpu.VMEM((count * rows, width), jnp.bfloat16),
            pltpu.VMEM((1, 128), jnp.float32),
            pltpu.SemaphoreType.DMA((2 * half - 1,)),
            pltpu.SemaphoreType.DMA((2, half, SUBS)),
            pltpu.SemaphoreType.DMA((2, half, SUBS)),
            pltpu.SemaphoreType.DMA((4,)),
            pltpu.SemaphoreType.DMA,
            pltpu.SemaphoreType.DMA((PARTS,)),
            pltpu.SemaphoreType.DMA,
            pltpu.SemaphoreType.DMA,
            pltpu.SemaphoreType.REGULAR,
        ],
        compiler_params=pltpu.CompilerParams(
            collective_id=0, has_side_effects=True, vmem_limit_bytes=53 * 2**20
        ),
    )(gradients, owners)


def solution(mesh):
    placed = (P("dp", "fsdp", None, None), P("dp", None))
    return jax.shard_map(
        on_device,
        mesh=mesh,
        in_specs=placed,
        out_specs=(P("fsdp", "dp", None), P("dp", "fsdp", None)),
        check_vma=False,
    )
```

```python
import functools

import jax
import jax.numpy as jnp
from jax import lax
from jax.experimental import pallas as pl
from jax.experimental.pallas import tpu as pltpu
from jax.sharding import PartitionSpec as P

MOST = 2
PARTS = 4
SUBS = 2 * PARTS
SLOTS = 4
PERIODS = 11
LANE = 128
LINES = 8
FAR_FIRST = (4, -3, 3, -2, 2, -1, 1, 0)
ACROSS = 4
CORES = 2
MESH = pl.DeviceIdType.MESH


def product(left_side, right_side):
    return jnp.dot(left_side, right_side, preferred_element_type=jnp.float32)


def fives(size):
    shape = (size, size)
    down = lax.broadcasted_iota(jnp.int32, shape, 0)
    across = lax.broadcasted_iota(jnp.int32, shape, 1)
    return jnp.where(down == across, 5.0, 0.0)


def within(index, count):
    return jnp.where(index >= count, index - count, index)


def wave_of(device):
    core = lax.rem(device, CORES)
    chip = lax.div(device, CORES)
    column, row = lax.rem(chip, ACROSS), lax.div(chip, ACROSS)
    return CORES * core + lax.rem(column + row, 2), row * (ACROSS // 2) + lax.div(column, 2)


def each_receiver(part, device, batch, send):
    core, parity = lax.div(part, CORES), lax.rem(part, CORES)
    chip = lax.div(device, CORES)
    first, mine = lax.div(lax.rem(chip, ACROSS), 2), lax.div(chip, ACROSS)
    even = lax.rem(parity + mine, 2)
    for offset in FAR_FIRST[2 * batch : 2 * batch + 2]:
        row = within(mine + offset % LINES, LINES)
        odd = 1 - even if offset % 2 else even
        for pair in (first, 1 - first):
            column = 2 * pair + odd
            send(row * (ACROSS // 2) + pair, (row * ACROSS + column) * CORES + core, offset == 0)


def blocks_stepped(index):
    lane, row = index >> 3, index & 7
    core, column = lane & 1, lane >> 1
    wave = 2 * core + ((column + row) & 1)
    return wave * 16 + row * 2 + (column >> 1)


def step_kernel(
    planes, count, x_ref, owners_ref, out_ref, slots_ref,
    own, come, turned, ready, gathered, back, returned, scale_mine, column_scales, scales, restored,
    block, scaled_low, first_step, step_square, partial_term, second_step, root, half_applied,
    grad_squares,
    load_sem, send_sem, recv_sem, push_sem, block_sem, row_sem, column_sem, scale_sem, plane_sem,
):
    plane = lax.axis_index("dp")
    me = lax.axis_index("fsdp")
    half = planes // 2
    group = count
    part_size = group // PARTS
    rows, width = out_ref.shape[0], out_ref.shape[2] // 2
    few = rows // 2
    lanes = ACROSS * CORES
    lines = count // lanes
    my_line, my_lane = lax.div(me, lanes), lax.rem(me, lanes)
    my_wave, my_place = wave_of(me)
    my_block = my_wave * part_size + my_place
    barrier = pltpu.get_barrier_semaphore()

    goals = [
        [within(plane + (far if way == 0 else planes - far), planes) for far in range(half + 1)]
        for way in (0, 1)
    ]

    def goal(way, far):
        return goals[way][far]

    def blocks(part):
        return pl.ds(pl.multiple_of(part * part_size, part_size), part_size)

    def place_of(sub):
        return pl.ds(lax.rem(sub, 2) * few, few), lax.div(sub, 2)

    def raw(way, far, sub):
        lines_of, part = place_of(sub)
        first = pl.multiple_of(goal(way, far) * group + part * part_size, part_size)
        return x_ref.at[0, lines_of, pl.ds(first, part_size), :]

    def slot(way, far):
        return 0 if far == 0 else far + way * (half - 1)

    def kept(way, far, sub):
        lines_of, part = place_of(sub)
        return own.at[slot(way, far), lines_of, blocks(part), :]

    def landed(way, far, sub):
        lines_of, part = place_of(sub)
        return come.at[way, far - 1, lines_of, blocks(part), :]

    def copy(way, far, sub, source):
        return pltpu.make_async_remote_copy(
            src_ref=source,
            dst_ref=landed(way, far, sub),
            send_sem=send_sem.at[way, far - 1, sub],
            recv_sem=recv_sem.at[way, far - 1, sub],
            device_id=(goal(way, 1), me),
            device_id_type=MESH,
        )

    def arrived(way, far, sub):
        copy(way, far, sub, landed(way, far, sub)).wait_recv()

    def load(way, far):
        first, size = (way * few, few) if far == half - 1 else (0, rows)
        start = pl.multiple_of(goal(way, far) * group, group)
        return pltpu.make_async_copy(
            x_ref.at[0, pl.ds(first, size), pl.ds(start, group), :],
            own.at[slot(way, far), pl.ds(first, size), :, :],
            load_sem.at[slot(way, far)],
        )

    def relay(way, far, sub):
        arrived(way, far + 1, sub)
        mine = kept(way, far, sub)
        total = mine[...].astype(jnp.float32) + landed(way, far + 1, sub)[...].astype(jnp.float32)
        mine[...] = total.astype(jnp.bfloat16)
        copy(way, far, sub, mine).start()

    def first_relay(sub):
        far = half - 1
        for way in (0, 1):

            @pl.when(lax.rem(sub, 2) != way)
            def _():
                copy(way, far, sub, raw(way, far, sub)).start()
                relay(1 - way, far, sub)

    def push(source, target, other, sent, got):
        pltpu.make_async_remote_copy(
            src_ref=source,
            dst_ref=target,
            send_sem=sent,
            recv_sem=got,
            device_id=(plane, other),
            device_id_type=MESH,
        ).start()

    def settle(buffer, semaphore):
        pltpu.make_async_copy(buffer, buffer, semaphore).wait()

    def in_column(step):
        return within(me + step * lanes, count)

    def in_row(step):
        return my_line * lanes + within(my_lane + step, lanes)

    def finish(sub):
        arrived(0, 1, sub)
        arrived(1, 1, sub)
        total = kept(0, 0, sub)[...].astype(jnp.float32)
        total += landed(0, 1, sub)[...].astype(jnp.float32)
        total += landed(1, 1, sub)[...].astype(jnp.float32)
        flat = total.reshape(few * part_size, 2 * width)
        tiles = [turned.at[tile] for tile in range(2 * width // LANE)]
        start = pl.multiple_of(lax.rem(sub, 2) * (few * part_size), few * part_size)
        for tile, lane in enumerate(tiles):
            lane[pl.ds(start, few * part_size), :] = flat[:, tile * LANE : (tile + 1) * LANE]

        @pl.when(lax.rem(sub, 2) == 1)
        def _():
            part = lax.div(sub, 2)
            for index in range(part_size):
                pieces = [lane[pl.ds(index, rows, stride=part_size), :] for lane in tiles]
                message = [
                    jnp.concatenate(pieces[: len(pieces) // 2], axis=1),
                    jnp.concatenate(pieces[len(pieces) // 2 :], axis=1),
                ]
                ready[part * part_size + index] = jnp.concatenate(message, axis=0).astype(
                    jnp.bfloat16
                )

    def hand_out(part, batch):
        def send(place, other, own_row):
            source = ready.at[part * part_size + place]

            def over():
                push(source, gathered.at[me], other, push_sem.at[0], block_sem)

            if not own_row:
                over()
                return
            pl.when(other != me)(over)

            @pl.when(other == me)
            def _():
                pltpu.make_async_copy(source, gathered.at[me], block_sem).start()

        each_receiver(part, me, batch, send)

    size = count * rows

    def take_block():
        settle(gathered, block_sem)
        received = gathered[...].astype(jnp.float32)
        sides = [received[:, :rows, :], received[:, rows:, :]]
        whole = jnp.concatenate([side.reshape(size, width) for side in sides], axis=1)
        grad_squares[...] = jnp.broadcast_to(
            jnp.sum(whole * whole, keepdims=True), grad_squares.shape
        )
        block[...] = whole.astype(jnp.bfloat16)

    def take_factor():
        factor = lax.dot_general(
            block[...], block[...], (((1,), (1,)), ((), ())), preferred_element_type=jnp.float32
        )
        scaled = factor * (1.0 / jnp.sqrt(jnp.sum(factor * factor, keepdims=True) + 1e-06))
        scaled_low[...] = scaled.astype(jnp.bfloat16)
        first_step[...] = ((fives(size) - scaled) * 0.25).astype(jnp.bfloat16)

    def take_square():
        step_square[...] = product(first_step[...], first_step[...]).astype(jnp.bfloat16)

    def take_partial():
        partial_term[...] = product(step_square[...], scaled_low[...]).astype(jnp.bfloat16)

    def take_second():
        next_scaled = product(step_square[...], partial_term[...])
        second_step[...] = ((fives(size) - next_scaled) * 0.25).astype(jnp.bfloat16)

    def take_root():
        root[...] = product(first_step[...], second_step[...]).astype(jnp.bfloat16)

    def take_half():
        half_applied[...] = product(root[...], block[...]).astype(jnp.bfloat16)

    def take_direction():
        direction = product(root[...], half_applied[...])
        graft = jnp.sqrt(grad_squares[...][:, :1]) / jnp.sqrt(
            jnp.sum(direction * direction, keepdims=True) + 1e-06
        )
        update = direction * graft
        sides = [update[:, :width], update[:, width:]]
        back[...] = jnp.concatenate(
            [side.reshape(count, rows, width) for side in sides], axis=1
        ).astype(jnp.bfloat16)
        scale_mine[...] = jnp.broadcast_to(graft, scale_mine.shape)

    def give_scale():
        def line(step, carry):
            push(scale_mine, column_scales.at[my_line], in_column(step), push_sem.at[2], column_sem)
            return carry

        lax.fori_loop(1, lines, line, 0)
        pltpu.make_async_copy(scale_mine, column_scales.at[my_line], column_sem).start()
        pltpu.make_async_copy(back.at[me], returned.at[my_block], row_sem.at[my_wave]).start()

    def give_rows(quarter):
        for step in range(quarter * lanes // 4, (quarter + 1) * lanes // 4):
            lane = within(my_lane + step, lanes)
            for offset in FAR_FIRST:
                if step or offset:
                    other = within(my_line + offset % lines, lines) * lanes + lane
                    push(
                        back.at[other], returned.at[my_block], other,
                        push_sem.at[1], row_sem.at[my_wave],
                    )

    def first_rows():
        give_scale()
        give_rows(0)

    stages = [
        take_block, take_factor, take_square, take_partial, take_second, take_root, take_half,
        take_direction, first_rows, *[functools.partial(give_rows, q) for q in (1, 2, 3)],
    ]

    loads = [load(way, far) for far in range(half - 1, 0, -1) for way in (0, 1)] + [load(0, 0)]
    for each in loads:
        each.start()
    def signal(semaphore, device):
        pl.semaphore_signal(semaphore, inc=1, device_id=device, device_id_type=MESH)

    def greet_column(step, carry):
        signal(barrier, (plane, in_column(step)))
        return carry

    def greet_row(step, carry):
        signal(barrier, (plane, in_row(step)))
        return carry

    def vouch(step, carry):
        signal(plane_sem, (plane, in_row(step)))
        return carry

    signal(barrier, (goal(0, 1), me))
    signal(barrier, (goal(1, 1), me))
    lax.fori_loop(1, lines, greet_column, 0)
    lax.fori_loop(1, lanes, greet_row, 0)
    pl.semaphore_wait(barrier, lines + lanes)

    def start_half_way(pair, carry):
        for way in (0, 1):
            sub = 2 * pair + way
            copy(way, half, sub, raw(way, half, sub)).start()
        return carry

    lax.fori_loop(0, SUBS // 2, start_half_way, 0)
    lax.fori_loop(1, lanes, vouch, 0)
    for each in loads:
        each.wait()
    first_relay(0)
    pl.semaphore_wait(plane_sem, lanes - 1)
    def period(now, carry):
        for turn in range(SLOTS):
            far = SLOTS - 1 - turn
            if far < half:
                lag = -1 if far == half - 1 else half - 1 - far
                sub = now - lag

                @pl.when((sub >= 0) & (sub < SUBS))
                def _():
                    if far == half - 1:
                        first_relay(sub)
                    elif far > 0:
                        relay(0, far, sub)
                        relay(1, far, sub)
                    else:
                        finish(sub)

            lag = half - 1 + (0 if turn == SLOTS - 1 else 1)
            last = now - lag

            @pl.when((last >= 0) & (last < SUBS - 1) & (lax.rem(last + SUBS, 2) == 1))
            def _():
                hand_out(lax.div(last, 2), (turn + 1) % SLOTS)

        return carry

    lax.fori_loop(0, PERIODS, period, 0)
    for batch in range(SLOTS):
        hand_out(PARTS - 1, batch)
    for stage in stages:
        stage()

    settle(column_scales, column_sem)
    mine_there = scales.at[pl.ds(my_lane * lines, lines)]

    def spread(step, carry):
        push(column_scales, mine_there, in_row(step), push_sem.at[3], scale_sem)
        return carry

    lax.fori_loop(1, lanes, spread, 0)
    pltpu.make_async_copy(column_scales, mine_there, scale_sem).start()

    def sent(pair, carry):
        for way in (0, 1):
            copy(way, half, 2 * pair + way, landed(way, half, 2 * pair + way)).wait_send()
            for far in range(1, half):
                for sub in (2 * pair, 2 * pair + 1):
                    copy(way, far, sub, landed(way, far, sub)).wait_send()
        return carry

    lax.fori_loop(0, SUBS // 2, sent, 0)
    settle(ready.at[pl.ds(0, count - 1)], push_sem.at[0])
    def restore(part, carry):
        settle(returned.at[blocks(part)], row_sem.at[part])
        flat = returned[blocks(part)].astype(jnp.float32).reshape(part_size * 2 * rows, width)
        for tile in range(width // LANE):
            lane = restored.at[tile]
            lane[...] = flat[:, tile * LANE : (tile + 1) * LANE]
            for side in range(2):
                first = side * width + tile * LANE
                for row in range(rows):
                    column = lane[pl.ds(side * rows + row, part_size, stride=2 * rows), :]
                    out_ref[row, blocks(part), first : first + LANE] = column.astype(jnp.bfloat16)
        return carry

    lax.fori_loop(0, PARTS - 1, restore, 0)
    settle(scales, scale_sem)
    factors = scales[...][:, 0, :1]
    square = (count, count)
    mine = jnp.broadcast_to((owners_ref[...] == me).astype(jnp.float32), square)
    stepped = blocks_stepped(lax.broadcasted_iota(jnp.int32, square, 0))
    across = lax.broadcasted_iota(jnp.int32, square, 1)
    owned = jnp.sum(jnp.where(across == stepped, mine, 0.0), axis=1, keepdims=True)
    earlier = jnp.sum(jnp.where(across < stepped, mine, 0.0), axis=1, keepdims=True)
    place = lax.broadcasted_iota(jnp.int32, (count, MOST), 1).astype(jnp.float32)
    picked = jnp.where((earlier == place) & (owned > 0.5), factors, 0.0)
    slots_ref[0] = jnp.sum(picked, axis=0, keepdims=True)
    restore(PARTS - 1, 0)

    settle(back.at[pl.ds(0, count - 1)], push_sem.at[1])
    settle(column_scales.at[pl.ds(0, lines - 1)], push_sem.at[2])
    settle(scales.at[pl.ds(0, (lanes - 1) * lines)], push_sem.at[3])


def on_device(gradients, owners):
    planes, count = lax.axis_size("dp"), lax.axis_size("fsdp")
    _, rows, blocks, width = gradients.shape
    group = blocks // planes
    half = planes // 2
    part_size = group // PARTS
    lines = count // (ACROSS * CORES)
    message = (group, 2 * rows, width // 2)
    matrix = (count * rows, count * rows)
    vmem = pl.BlockSpec(memory_space=pltpu.VMEM)
    return pl.pallas_call(
        functools.partial(step_kernel, planes, count),
        out_shape=(
            jax.ShapeDtypeStruct((rows, group, width), jnp.bfloat16),
            jax.ShapeDtypeStruct((1, 1, MOST), jnp.float32),
        ),
        in_specs=[pl.BlockSpec(memory_space=pltpu.HBM), vmem],
        out_specs=(vmem, vmem),
        scratch_shapes=[
            pltpu.VMEM((2 * half - 1, rows, group, width), jnp.bfloat16),
            pltpu.VMEM((2, half, rows, group, width), jnp.bfloat16),
            pltpu.VMEM((width // LANE, rows * part_size, LANE), jnp.float32),
            *[pltpu.VMEM(message, jnp.bfloat16)] * 4,
            pltpu.VMEM((1, 128), jnp.float32),
            pltpu.VMEM((lines, 1, 128), jnp.float32),
            pltpu.VMEM((count, 1, 128), jnp.float32),
            pltpu.VMEM((width // 2 // LANE, part_size * 2 * rows, LANE), jnp.float32),
            pltpu.VMEM((count * rows, width), jnp.bfloat16),
            *[pltpu.VMEM(matrix, jnp.bfloat16)] * 6,
            pltpu.VMEM((count * rows, width), jnp.bfloat16),
            pltpu.VMEM((1, 128), jnp.float32),
            pltpu.SemaphoreType.DMA((2 * half - 1,)),
            pltpu.SemaphoreType.DMA((2, half, SUBS)),
            pltpu.SemaphoreType.DMA((2, half, SUBS)),
            pltpu.SemaphoreType.DMA((4,)),
            pltpu.SemaphoreType.DMA,
            pltpu.SemaphoreType.DMA((PARTS,)),
            pltpu.SemaphoreType.DMA,
            pltpu.SemaphoreType.DMA,
            pltpu.SemaphoreType.REGULAR,
        ],
        compiler_params=pltpu.CompilerParams(
            collective_id=0, has_side_effects=True, vmem_limit_bytes=53 * 2**20
        ),
    )(gradients, owners)


def solution(mesh):
    placed = (P("dp", "fsdp", None, None), P("dp", None))
    return jax.shard_map(
        on_device,
        mesh=mesh,
        in_specs=placed,
        out_specs=(P("fsdp", "dp", None), P("dp", "fsdp", None)),
        check_vma=False,
    )
```
